32 devices in a mesh: pair: 32 (over z, y, x, core), sigma: 1.
Axes of the slice: x: 2, y: 2, z: 4, core: 2. Of those that a mesh axis runs over, the one named last changes fastest.
Arguments:
- pair_density_matrices: bfloat16 [65536, 1536], P('pair'), may hold values from -6 to 6
- energy_bins: int32 [65536, 2], P('pair'), may hold values from 0 to 63
- bin_weights: float32 [2, 64], replicated, may hold values from 0.05 to 1
- coulomb: float32 [1536], replicated, may hold values from 0.5 to 4
- state_matrices: bfloat16 [1536, 2048], P(None, 'sigma'), may hold values from -6 to 6
Outputs:
- screened_states: float32 [1536, 2, 2048], P('pair', None, 'sigma')
- sigma_diag: float32 [2, 2048], P(None, 'sigma')
The draws below stay inside these ranges and needn't reach their ends.
All inputs are finite; a program needn't handle non-finite values.
Results may differ from the reference program's by a relative error of at most 0.00035.
Values sent between devices are 32-bit elements; how exact they have to be, the bound alone decides.
A program may use at most 128 MiB of HBM per device.

```python
import math
import jax
import jax.numpy as jnp
from jax import lax

NG = 1536
NS = 2048
NF = 2
NBIN = 64
PAIRS = 65536


def set_ends(values, key, least, top_value):
    index_at = [jax.random.randint(jax.random.fold_in(key, axis), (), 0, length) for axis, length in enumerate(values.shape)]
    main_axis = values.shape.index(max(values.shape))
    beside = index_at[:main_axis] + [(index_at[main_axis] + 1) % values.shape[main_axis]] + index_at[main_axis + 1:]
    return values.at[tuple(index_at)].set(least).at[tuple(beside)].set(top_value)


def with_spikes(values, stream_key, source, target, parts, factor):
    def block_of(position):
        return (jnp.arange(values.shape[position]) // (values.shape[position] // parts)).reshape((-1,) + (1,) * (values.ndim - 1 - position))

    one_side = jax.random.permutation(stream_key, parts)[block_of(target)]
    far = (block_of(target) + parts // 2) % parts
    return jnp.where((block_of(source) == one_side) | (block_of(source) == far), factor * values, values)


def block_levels(key, extent, pieces, least, high):
    level = 1.0
    for axis_at, parts in pieces:
        heights = jax.random.uniform(jax.random.fold_in(jax.random.fold_in(key, 6), axis_at), (parts,), jnp.float32, least / len(pieces), high / len(pieces))
        level = level * jnp.repeat(jnp.exp(heights), extent[axis_at] // parts).reshape((-1,) + (1,) * (len(extent) - 1 - axis_at))
    return level


def bell_draw(own_key, shape, scale, most, split=(), kind=jnp.bfloat16):
    entries = scale * jax.random.normal(own_key, shape, jnp.float32)
    if split:
        entries = entries * block_levels(own_key, shape, split, -0.22, 0.18)
    return jnp.clip(entries, -most, most).astype(kind)


def heavy_noise(key, dims, width, bound, pieces, heavy, kind=jnp.bfloat16):
    values = width * jax.random.normal(key, dims, jnp.float32)
    if pieces:
        values = values * block_levels(key, dims, pieces, -0.22, 0.18)
    return jnp.clip(with_spikes(values, jax.random.fold_in(key, 3), *heavy), -bound, bound).astype(kind)


def setup_inputs(seed: int = 0) -> dict:
    key_of = jax.random.split(jax.random.key(seed), 6)
    return {
        "pair_density_matrices": heavy_noise(key_of[0], (PAIRS, NG), 1.0, 6.0, ((0, 32),), (0, 1, 32, 2.75)),
        "energy_bins": set_ends(jax.random.randint(key_of[1], (PAIRS, NF), 0, NBIN), jax.random.fold_in(key_of[1], 1), 0, NBIN - 1).astype(jnp.int32),
        "bin_weights": jnp.clip(jnp.exp(jax.random.uniform(key_of[2], (NF, NBIN), jnp.float32, math.log(0.05), math.log(1.0))), 0.05, 1.0),
        "coulomb": jnp.clip(jnp.exp(jax.random.uniform(key_of[3], (NG,), jnp.float32, math.log(0.5), math.log(4.0))), 0.5, 4.0),
        "state_matrices": bell_draw(key_of[4], (NG, NS), 1.0, 6.0),
    }


def reference(pair_density_matrices, energy_bins, bin_weights, coulomb, state_matrices):
    pair_total = pair_density_matrices.shape[0]
    freq_ids = jnp.arange(NF, dtype=jnp.int32)
    weight = bin_weights[freq_ids[None, :], energy_bins] / jnp.float32(pair_total)
    coulomb_root = jnp.sqrt(coulomb)
    pairs_wide = pair_density_matrices.astype(jnp.float32)
    states_wide = state_matrices.astype(jnp.float32)
    applied_list = []
    diagonal_entries_list = []
    for freq_index in range(NF):
        scaled_product = (weight[:, freq_index:freq_index + 1] * pairs_wide).astype(jnp.bfloat16)
        scaled_product = lax.optimization_barrier(scaled_product).astype(jnp.float32)
        polar = -jnp.dot(pairs_wide.T, scaled_product, precision=lax.Precision.HIGHEST)
        screened = coulomb_root[:, None] * polar * coulomb_root[None, :]
        applied = jnp.dot(screened, states_wide, precision=lax.Precision.HIGHEST)
        applied_list.append(applied)
        diagonal_entries_list.append(lax.optimization_barrier(jnp.sum(states_wide * applied, axis=0)) / jnp.float32(NG))
    screened_states = jnp.stack(applied_list, axis=1)
    sigma_diag = jnp.stack(diagonal_entries_list, axis=0)
    return (screened_states, sigma_diag)
```

```python
import functools

import jax
import jax.numpy as jnp
from jax import lax
from jax.experimental import pallas as pl
from jax.experimental.pallas import tpu as pltpu
from jax.sharding import PartitionSpec as P

MESH = pl.DeviceIdType.MESH
LANES = 128


def pair_weights(energy_bins, bin_weights, pair_total):
    bin_levels = jnp.arange(bin_weights.shape[1], dtype=jnp.int32)
    matches = (energy_bins[:, :, None] == bin_levels[None, None, :]).astype(jnp.float32)
    picked = jnp.sum(matches * bin_weights[None, :, :], axis=2)
    return picked / jnp.float32(pair_total)


def halving_orders(bits):
    first = list(range(bits))
    second = list(range(bits))
    if bits >= 4:
        first = [0, 1, 3, 2] + first[4:]
        second = [0, 2, 3, 1] + second[4:]
    return first, second


def place_in_order(block, order):
    place = 0
    for bit in order:
        place = place * 2 + ((block >> bit) & 1)
    return place


def flip(me, bit):
    own = lax.rem(me // (1 << bit), 2)
    return own, me + (1 << bit) * (1 - 2 * own)


def greet(me, bits):
    barrier = pltpu.get_barrier_semaphore()
    for bit in range(bits):
        pl.semaphore_signal(
            barrier, inc=1, device_id={"pair": flip(me, bit)[1]}, device_id_type=MESH
        )
    pl.semaphore_wait(barrier, bits)


def polar_kernel(bits, orders, lags, rows_ref, cols_ref, weight_ref, out_ref,
                 spread, scaled, prod, *rest):
    recv = rest[:bits]
    send_sem, recv_sem = rest[bits:]
    me = lax.axis_index("pair")
    freqs = len(orders)
    pairs, width = cols_ref.shape
    steps = width // LANES
    rows = out_ref.shape[1]
    half = (1 << bits) // 2
    piece = 256

    greet(me, bits)
    for f in range(freqs):
        spread[:, f * LANES:(f + 1) * LANES] = jnp.broadcast_to(
            weight_ref[:, f:f + 1], (pairs, LANES)
        )

    offsets = []
    for order in orders:
        at, found = 0, [0]
        for stage, bit in enumerate(order):
            at = at + flip(me, bit)[0] * ((1 << bits) >> (stage + 1))
            found.append(at)
        offsets.append(found)

    def copy_of(f, stage, t):
        bit = orders[f][stage]
        own, partner = flip(me, bit)
        size = (1 << bits) >> (stage + 1)
        start = offsets[f][stage] + (1 - own) * size
        return pltpu.make_async_remote_copy(
            src_ref=prod.at[f, t, pl.ds(start, size)],
            dst_ref=recv[stage].at[f, t],
            send_sem=send_sem.at[f, stage, t],
            recv_sem=recv_sem.at[f, stage, t],
            device_id={"pair": partner},
            device_id_type=MESH,
        )

    core = flip(me, 0)[0]

    def multiply(side, t):
        product = jnp.dot(rows_ref[side], scaled[...], preferred_element_type=jnp.float32)
        for k in range(half):
            for f in range(freqs):
                low = place_in_order(2 * k, orders[f])
                prod[f, t, low + side * half] = product[
                    k * rows:(k + 1) * rows, f * LANES:(f + 1) * LANES
                ]

    def body(step, carry):
        @pl.when(step < steps)
        def _():
            cols = pl.ds(pl.multiple_of(step * LANES, LANES), LANES)

            def scale(i, c):
                at = pl.ds(pl.multiple_of(i * piece, piece), piece)
                wide = cols_ref[at, cols].astype(jnp.float32)
                for f in range(freqs):
                    lane = slice(f * LANES, (f + 1) * LANES)
                    scaled[at, lane] = (spread[at, lane] * wide).astype(jnp.bfloat16)
                return c

            lax.fori_loop(0, pairs // piece, scale, 0)
            multiply(1 - core, step)
            for f in range(freqs):
                copy_of(f, 0, step).start()
            multiply(core, step)

        for stage in range(1, bits + 1):
            t = step - lags[stage]

            @pl.when(jnp.logical_and(t >= 0, t < steps))
            def _(stage=stage, t=t):
                size = (1 << bits) >> stage
                for f in range(freqs):
                    copy_of(f, stage - 1, t).wait_recv()
                    kept = pl.ds(offsets[f][stage], size)
                    if stage < bits:
                        prod[f, t, kept] += recv[stage - 1][f, t]
                        copy_of(f, stage, t).start()
                    else:
                        cols = pl.ds(pl.multiple_of(t * LANES, LANES), LANES)
                        out_ref[f, :, cols] = (
                            prod[f, t, offsets[f][stage]] + recv[stage - 1][f, t, 0]
                        )

        return carry

    lax.fori_loop(0, steps + lags[bits], body, 0)

    def finish(t, carry):
        for stage in range(bits):
            for f in range(freqs):
                copy_of(f, stage, t).wait_send()
        return carry

    lax.fori_loop(0, steps, finish, 0)


def polar_rows(pair_rows, columns, weight, pair_count):
    pairs, width = columns.shape
    total_rows = pair_rows.shape[1]
    freqs = weight.shape[1]
    bits = pair_count.bit_length() - 1
    rows = total_rows // pair_count
    steps = width // LANES
    orders = halving_orders(bits)
    lags = [0, 1] + [2 * k + 1 for k in range(1, bits)]
    by_core = pair_rows.reshape(pairs, pair_count // 2, 2, rows).transpose(2, 1, 3, 0)
    by_core = by_core.reshape(2, total_rows // 2, pairs)
    return pl.pallas_call(
        functools.partial(polar_kernel, bits, orders, lags),
        out_shape=jax.ShapeDtypeStruct((freqs, rows, width), jnp.float32),
        in_specs=[pl.BlockSpec(memory_space=pltpu.VMEM)] * 3,
        out_specs=pl.BlockSpec(memory_space=pltpu.VMEM),
        scratch_shapes=[
            pltpu.VMEM((pairs, freqs * LANES), jnp.float32),
            pltpu.VMEM((pairs, freqs * LANES), jnp.bfloat16),
            pltpu.VMEM((freqs, steps, pair_count, rows, LANES), jnp.float32),
        ]
        + [
            pltpu.VMEM((freqs, steps, pair_count >> (s + 1), rows, LANES), jnp.float32)
            for s in range(bits)
        ]
        + [
            pltpu.SemaphoreType.DMA((freqs, bits, steps)),
            pltpu.SemaphoreType.DMA((freqs, bits, steps)),
        ],
        compiler_params=pltpu.CompilerParams(
            collective_id=0, has_side_effects=True, vmem_limit_bytes=60 * 1024 * 1024
        ),
        cost_estimate=pl.CostEstimate(
            flops=2 * pairs * total_rows * width * freqs,
            bytes_accessed=4 * pairs * total_rows,
            transcendentals=0,
        ),
    )(by_core, columns, weight)


def total_kernel(bits, part_ref, out_ref, held, got, send_sem, recv_sem):
    me = lax.axis_index("pair")
    greet(me, bits)
    held[0] = part_ref[...]
    for bit in range(bits):
        copy = pltpu.make_async_remote_copy(
            src_ref=held.at[bit],
            dst_ref=got.at[bit],
            send_sem=send_sem.at[bit],
            recv_sem=recv_sem.at[bit],
            device_id={"pair": flip(me, bit)[1]},
            device_id_type=MESH,
        )
        copy.start()
        copy.wait()
        held[bit + 1] = held[bit] + got[bit]
    out_ref[...] = held[bits]


def pair_total(part, pair_count):
    bits = pair_count.bit_length() - 1
    return pl.pallas_call(
        functools.partial(total_kernel, bits),
        out_shape=jax.ShapeDtypeStruct(part.shape, jnp.float32),
        in_specs=[pl.BlockSpec(memory_space=pltpu.VMEM)],
        out_specs=pl.BlockSpec(memory_space=pltpu.VMEM),
        scratch_shapes=[
            pltpu.VMEM((bits + 1,) + part.shape, jnp.float32),
            pltpu.VMEM((bits,) + part.shape, jnp.float32),
            pltpu.SemaphoreType.DMA((bits,)),
            pltpu.SemaphoreType.DMA((bits,)),
        ],
        compiler_params=pltpu.CompilerParams(collective_id=1, has_side_effects=True),
    )(part)


def local(pair_density_matrices, energy_bins, bin_weights, coulomb, state_matrices):
    pair_local, width = pair_density_matrices.shape
    pair_count = lax.axis_size("pair")
    self_energy_count = lax.axis_size("sigma")
    row_count = width // pair_count
    col_count = width // self_energy_count
    pair_position = lax.axis_index("pair")
    sigma_pos = lax.axis_index("sigma")
    weight = pair_weights(energy_bins, bin_weights, pair_local * pair_count)
    column_slab = lax.dynamic_slice_in_dim(
        pair_density_matrices, sigma_pos * col_count, col_count, 1
    )
    polar_block = -polar_rows(pair_density_matrices, column_slab, weight, pair_count)
    coulomb_root = jnp.sqrt(coulomb)
    root_rows = lax.dynamic_slice_in_dim(coulomb_root, pair_position * row_count, row_count, 0)
    coulomb_root_columns = lax.dynamic_slice_in_dim(
        coulomb_root, sigma_pos * col_count, col_count, 0
    )
    screened = root_rows[None, :, None] * polar_block * coulomb_root_columns[None, None, :]
    states_wide = state_matrices.astype(jnp.float32)
    applied = jnp.einsum(
        "frc,cn->rfn",
        lax.all_gather(screened, "sigma", axis=2, tiled=True),
        states_wide,
        precision=lax.Precision.HIGHEST,
    )
    own_states = lax.dynamic_slice_in_dim(states_wide, pair_position * row_count, row_count, 0)
    partial_contribution = jnp.sum(own_states[:, None, :] * applied, axis=0) / jnp.float32(width)
    sigma_diag = pair_total(partial_contribution, pair_count)
    return (applied, sigma_diag)


def solution(mesh):
    return jax.shard_map(
        local,
        mesh=mesh,
        in_specs=(P("pair", None), P("pair", None), P(), P(), P(None, "sigma")),
        out_specs=(P("pair", None, "sigma"), P(None, "sigma")),
        check_vma=False,
    )
```

```python
import functools

import jax
import jax.numpy as jnp
from jax import lax
from jax.experimental import pallas as pl
from jax.experimental.pallas import tpu as pltpu
from jax.sharding import PartitionSpec as P

MESH = pl.DeviceIdType.MESH
LANES = 128


def pair_weights(energy_bins, bin_weights, pair_total):
    bin_levels = jnp.arange(bin_weights.shape[1], dtype=jnp.int32)
    matches = (energy_bins[:, :, None] == bin_levels[None, None, :]).astype(jnp.float32)
    picked = jnp.sum(matches * bin_weights[None, :, :], axis=2)
    return picked / jnp.float32(pair_total)


def halving_orders(bits):
    first = list(range(bits))
    second = list(range(bits))
    if bits >= 4:
        first = [0, 1, 3, 2] + first[4:]
        second = [0, 2, 3, 1] + second[4:]
    return first, second


def place_in_order(block, order):
    place = 0
    for bit in order:
        place = place * 2 + ((block >> bit) & 1)
    return place


def flip(me, bit):
    own = lax.rem(me // (1 << bit), 2)
    return own, me + (1 << bit) * (1 - 2 * own)


def greet(me, bits):
    barrier = pltpu.get_barrier_semaphore()
    for bit in range(bits):
        pl.semaphore_signal(
            barrier, inc=1, device_id={"pair": flip(me, bit)[1]}, device_id_type=MESH
        )
    pl.semaphore_wait(barrier, bits)


def polar_kernel(bits, orders, lags, slab, full_ref, *refs):
    if slab is None:
        cols_ref = full_ref
    else:
        cols_ref, *refs = refs
    weight_ref, out_ref, spread, scaled, turned, prod, *rest = refs
    recv = rest[:bits]
    send_sem, recv_sem = rest[bits:]
    me = lax.axis_index("pair")
    freqs = len(orders)
    pairs, width = cols_ref.shape
    steps = width // LANES
    rows = out_ref.shape[1]
    half = (1 << bits) // 2
    half_rows = half * rows
    piece = 256

    greet(me, bits)
    def turn(i, c):
        lane = pl.ds(pl.multiple_of(i * LANES, LANES), LANES)
        turned[lane, :] = full_ref[:, lane].T
        return c

    lax.fori_loop(0, full_ref.shape[1] // LANES, turn, 0)
    for f in range(freqs):
        spread[:, f * LANES:(f + 1) * LANES] = jnp.broadcast_to(
            weight_ref[:, f:f + 1], (pairs, LANES)
        )

    offsets = []
    for order in orders:
        at, found = 0, [0]
        for stage, bit in enumerate(order):
            at = at + flip(me, bit)[0] * ((1 << bits) >> (stage + 1))
            found.append(at)
        offsets.append(found)

    def copy_of(f, stage, t):
        bit = orders[f][stage]
        own, partner = flip(me, bit)
        size = (1 << bits) >> (stage + 1)
        start = offsets[f][stage] + (1 - own) * size
        return pltpu.make_async_remote_copy(
            src_ref=prod.at[f, t, pl.ds(start, size)],
            dst_ref=recv[stage].at[f, t],
            send_sem=send_sem.at[f, stage, t],
            recv_sem=recv_sem.at[f, stage, t],
            device_id={"pair": partner},
            device_id_type=MESH,
        )

    def multiply(side, t):
        product = jnp.dot(
            turned[side * half_rows:(side + 1) * half_rows, :],
            scaled[...],
            preferred_element_type=jnp.float32,
        )
        for k in range(half):
            for f in range(freqs):
                prod[f, t, place_in_order(side * half + k, orders[f])] = product[
                    k * rows:(k + 1) * rows, f * LANES:(f + 1) * LANES
                ]

    def body(step, carry):
        @pl.when(step < steps)
        def _():
            cols = pl.ds(pl.multiple_of(step * LANES, LANES), LANES)

            def scale(i, c):
                at = pl.ds(pl.multiple_of(i * piece, piece), piece)
                wide = cols_ref[at, cols].astype(jnp.float32)
                for f in range(freqs):
                    lane = slice(f * LANES, (f + 1) * LANES)
                    scaled[at, lane] = (spread[at, lane] * wide).astype(jnp.bfloat16)
                return c

            lax.fori_loop(0, pairs // piece, scale, 0)
            multiply(0, step)
            multiply(1, step)
            for f in range(freqs):
                copy_of(f, 0, step).start()

        for stage in range(1, bits + 1):
            t = step - lags[stage]

            @pl.when(jnp.logical_and(t >= 0, t < steps))
            def _(stage=stage, t=t):
                size = (1 << bits) >> stage
                for f in range(freqs):
                    copy_of(f, stage - 1, t).wait_recv()
                    kept = pl.ds(offsets[f][stage], size)
                    if stage < bits:
                        prod[f, t, kept] += recv[stage - 1][f, t]
                        copy_of(f, stage, t).start()
                    else:
                        cols = pl.ds(pl.multiple_of(t * LANES, LANES), LANES)
                        out_ref[f, :, cols] = (
                            prod[f, t, offsets[f][stage]] + recv[stage - 1][f, t, 0]
                        )

        return carry

    lax.fori_loop(0, steps + lags[bits], body, 0)

    def finish(t, carry):
        for stage in range(bits):
            for f in range(freqs):
                copy_of(f, stage, t).wait_send()
        return carry

    lax.fori_loop(0, steps, finish, 0)


def polar_rows(densities, slab, weight, pair_count):
    pairs, total_rows = densities.shape
    operands = [densities, weight] if slab is None else [densities, slab, weight]
    width = total_rows if slab is None else slab.shape[1]
    freqs = weight.shape[1]
    bits = pair_count.bit_length() - 1
    rows = total_rows // pair_count
    steps = width // LANES
    orders = halving_orders(bits)
    lags = [0, 1] + [k + 2 for k in range(1, bits)]
    return pl.pallas_call(
        functools.partial(polar_kernel, bits, orders, lags, None if slab is None else 0),
        out_shape=jax.ShapeDtypeStruct((freqs, rows, width), jnp.float32),
        in_specs=[pl.BlockSpec(memory_space=pltpu.VMEM)] * len(operands),
        out_specs=pl.BlockSpec(memory_space=pltpu.VMEM),
        scratch_shapes=[
            pltpu.VMEM((pairs, freqs * LANES), jnp.float32),
            pltpu.VMEM((pairs, freqs * LANES), jnp.bfloat16),
            pltpu.VMEM((total_rows, pairs), jnp.bfloat16),
            pltpu.VMEM((freqs, steps, pair_count, rows, LANES), jnp.float32),
        ]
        + [
            pltpu.VMEM((freqs, steps, pair_count >> (s + 1), rows, LANES), jnp.float32)
            for s in range(bits)
        ]
        + [
            pltpu.SemaphoreType.DMA((freqs, bits, steps)),
            pltpu.SemaphoreType.DMA((freqs, bits, steps)),
        ],
        compiler_params=pltpu.CompilerParams(
            collective_id=0, has_side_effects=True, vmem_limit_bytes=60 * 1024 * 1024
        ),
        cost_estimate=pl.CostEstimate(
            flops=2 * pairs * total_rows * width * freqs,
            bytes_accessed=4 * pairs * total_rows,
            transcendentals=0,
        ),
    )(*operands)


def total_kernel(near, far, part_ref, out_ref, held, got, got_far, send_sem, recv_sem):
    me = lax.axis_index("pair")
    low, high = lax.rem(me, near), me // near
    groups = []
    for k in range(1, near):
        slot = lax.rem(low + k, near)
        groups.append((slot, high * near + slot))
    groups_far = []
    for k in range(1, far):
        slot = lax.rem(high + k, far)
        groups_far.append((slot, slot * near + low))

    barrier = pltpu.get_barrier_semaphore()
    for _, peer in groups + groups_far:
        pl.semaphore_signal(barrier, inc=1, device_id={"pair": peer}, device_id_type=MESH)
    pl.semaphore_wait(barrier, near + far - 2)

    def exchange(source, slots, own, peers, base):
        copies = []
        for k, (slot, peer) in enumerate(peers):
            copies.append(
                pltpu.make_async_remote_copy(
                    src_ref=source,
                    dst_ref=slots.at[own],
                    send_sem=send_sem.at[base + k],
                    recv_sem=recv_sem.at[base + own],
                    device_id={"pair": peer},
                    device_id_type=MESH,
                )
            )
            copies[-1].start()
        slots[own] = source[...]
        for slot, _ in peers:
            pltpu.make_async_remote_copy(
                src_ref=source,
                dst_ref=slots.at[slot],
                send_sem=send_sem.at[base],
                recv_sem=recv_sem.at[base + slot],
                device_id={"pair": peers[0][1]},
                device_id_type=MESH,
            ).wait_recv()
        total = slots[0]
        for k in range(1, len(peers) + 1):
            total = total + slots[k]
        return total, copies

    total, copies = exchange(part_ref, got, low, groups, 0)
    held[...] = total
    total, more = exchange(held, got_far, high, groups_far, near)
    out_ref[...] = total
    for copy in copies + more:
        copy.wait_send()


def pair_total(part, pair_count):
    bits = pair_count.bit_length() - 1
    near = 1 << ((bits + 1) // 2)
    far = pair_count // near
    return pl.pallas_call(
        functools.partial(total_kernel, near, far),
        out_shape=jax.ShapeDtypeStruct(part.shape, jnp.float32),
        in_specs=[pl.BlockSpec(memory_space=pltpu.VMEM)],
        out_specs=pl.BlockSpec(memory_space=pltpu.VMEM),
        scratch_shapes=[
            pltpu.VMEM(part.shape, jnp.float32),
            pltpu.VMEM((near,) + part.shape, jnp.float32),
            pltpu.VMEM((far,) + part.shape, jnp.float32),
            pltpu.SemaphoreType.DMA((near + far,)),
            pltpu.SemaphoreType.DMA((near + far,)),
        ],
        compiler_params=pltpu.CompilerParams(collective_id=1, has_side_effects=True),
    )(part)


def local(pair_density_matrices, energy_bins, bin_weights, coulomb, state_matrices):
    pair_local, width = pair_density_matrices.shape
    pair_count = lax.axis_size("pair")
    self_energy_count = lax.axis_size("sigma")
    row_count = width // pair_count
    col_count = width // self_energy_count
    pair_position = lax.axis_index("pair")
    sigma_pos = lax.axis_index("sigma")
    weight = pair_weights(energy_bins, bin_weights, pair_local * pair_count)
    column_slab = lax.dynamic_slice_in_dim(
        pair_density_matrices, sigma_pos * col_count, col_count, 1
    ) if self_energy_count > 1 else None
    polar_block = -polar_rows(pair_density_matrices, column_slab, weight, pair_count)
    coulomb_root = jnp.sqrt(coulomb)
    root_rows = lax.dynamic_slice_in_dim(coulomb_root, pair_position * row_count, row_count, 0)
    coulomb_root_columns = lax.dynamic_slice_in_dim(
        coulomb_root, sigma_pos * col_count, col_count, 0
    )
    screened = root_rows[None, :, None] * polar_block * coulomb_root_columns[None, None, :]
    states_wide = state_matrices.astype(jnp.float32)
    applied = jnp.einsum(
        "frc,cn->rfn",
        lax.all_gather(screened, "sigma", axis=2, tiled=True),
        states_wide,
        precision=lax.Precision.HIGHEST,
    )
    own_states = lax.dynamic_slice_in_dim(states_wide, pair_position * row_count, row_count, 0)
    partial_contribution = jnp.sum(own_states[:, None, :] * applied, axis=0) / jnp.float32(width)
    sigma_diag = pair_total(partial_contribution, pair_count)
    return (applied, sigma_diag)


def solution(mesh):
    return jax.shard_map(
        local,
        mesh=mesh,
        in_specs=(P("pair", None), P("pair", None), P(), P(), P(None, "sigma")),
        out_specs=(P("pair", None, "sigma"), P(None, "sigma")),
        check_vma=False,
    )
```
